256 devices in a mesh: tok: 64 (over x_lo, z, y), head: 4 (over x_hi, core).
Axes of the slice: x: 4 (x_hi: 2, x_lo: 2; x = x_hi * 2 + x_lo), y: 4, z: 8, core: 2. Of those that a mesh axis runs over, the one named last changes fastest.
Arguments:
- queries: bfloat16 [16384, 24, 128], P('tok', 'head'), may hold values from -4.5 to 4.5
- keys: bfloat16 [16384, 24, 128], P('tok', 'head'), may hold values from -4.5 to 4.5
- values: bfloat16 [16384, 24, 128], P('tok', 'head'), may hold values from -5 to 5
- grad_out: bfloat16 [16384, 3072], P('tok', 'head'), may hold values from -6 to 6
- w_out: bfloat16 [3072, 3072], P('head'), may hold values from -0.109375 to 0.109375
- crit: int32 [64, 40], P('tok'), may hold values from -1 to 1023, as said below
Outputs:
- grad_q: bfloat16 [16384, 24, 128], P('tok', 'head')
- grad_k: bfloat16 [16384, 24, 128], P('tok', 'head')
- grad_v: bfloat16 [16384, 24, 128], P('tok', 'head')
The draws below stay inside these ranges and needn't reach their ends.
Inputs may be any that keep to these rules, and one draw needn't show every extreme that they name: `crit`: row b lists distinct key tiles, -1 marking unused entries, which come last; no listed tile lies in query block b - 1, b or b + 1 (not counted round); at most 1 tiles of one row lie in one query block, and some row has 1 tiles in one block; row 0 lists a tile of block 63 and row 63 a tile of block 0; some row has no unused entry, and every row uses half of its entries or more.
All inputs are finite; a program needn't handle non-finite values.
Results may differ from the reference program's by a relative error of at most 0.022.
Values may be sent and summed in bfloat16 or wider, within the bound.
No kernel may reach another device: no remote copies, remote signals or barrier semaphores. Data moves between devices by JAX's collectives and lax.ppermute only.
A program may use at most 128 MiB of HBM per device.

```python
import jax
import jax.numpy as jnp
from jax import lax

D = 3072
HEADS = 24
HDIM = 128
TOK_DEV = 256
KT = 16
NCRIT = 40
TOKENS = 16384


def draw_queries(key, part):
    key = jax.random.fold_in(key, 3)
    shape = (TOKENS, HEADS, HDIM)
    base = jnp.clip(jax.random.normal(key, shape, jnp.float32), -4.5, 4.5)
    return base.astype(jnp.bfloat16)


def draw_keys(key, part):
    key = jax.random.fold_in(key, 5)
    shape = (TOKENS, HEADS, HDIM)
    base = jnp.clip(jax.random.normal(key, shape, jnp.float32), -4.5, 4.5)
    return base.astype(jnp.bfloat16)


def draw_crit(key, part):
    key = jax.random.fold_in(key, 11)
    blocks = TOKENS // TOK_DEV
    per_block = TOK_DEV // KT
    far = blocks - 3
    capacity = (NCRIT + blocks - 4) // (blocks - 3)
    keys_a, key_b, keys_c, key_d, key_e = jax.random.split(key, 5)
    owner_perm = jax.vmap(lambda sub: jax.random.permutation(sub, far))(jax.random.split(keys_a, blocks))
    entry = jnp.arange(NCRIT)
    rank = entry // capacity
    slot = entry % capacity
    block_ids = jnp.arange(blocks)
    owner = (block_ids[:, None] + owner_perm[:, rank] + 2) % blocks
    first_rank = (rank == 0)[None, :]
    owner = jnp.where(first_rank & (block_ids[:, None] == 0), blocks - 1, owner)
    owner = jnp.where(first_rank & (block_ids[:, None] == blocks - 1), 0, owner)
    start = jax.random.randint(key_b, (blocks, far), 0, per_block)[:, rank]
    tiles = owner * per_block + (start + slot[None, :]) % per_block
    order = jax.vmap(lambda sub: jax.random.permutation(sub, NCRIT))(jax.random.split(keys_c, blocks))
    tiles = jnp.take_along_axis(tiles, order, axis=1)
    lengths = jax.random.randint(key_d, (blocks,), NCRIT // 2, NCRIT + 1)
    full_row = jax.random.randint(key_e, (), 0, blocks)
    lengths = jnp.where(block_ids == full_row, NCRIT, lengths)
    lengths = jnp.where((block_ids == 0) | (block_ids == blocks - 1), NCRIT, lengths)
    return jnp.where(entry[None, :] < lengths[:, None], tiles, -1).astype(jnp.int32)


def shard_levels(stream_key, shape, pieces, smallest, top_value):
    def one(axis_at, shards_of):
        heights = jax.random.uniform(jax.random.fold_in(jax.random.fold_in(stream_key, 6), axis_at), (shards_of,), jnp.float32, smallest / len(pieces), top_value / len(pieces))
        return jnp.repeat(jnp.exp(heights), shape[axis_at] // shards_of).reshape((-1,) + (1,) * (len(shape) - axis_at - 1))

    level = one(*pieces[0])
    for cut in pieces[1:]:
        level = level * one(*cut)
    return level


def centred(stream_key, shape, deviation, limit, cuts=(), held_as=jnp.bfloat16):
    result = jax.random.normal(stream_key, shape, jnp.float32) * deviation
    if len(cuts) > 0:
        result = shard_levels(stream_key, shape, cuts, -0.22, 0.18) * result
    return jnp.clip(result, min=-limit, max=limit).astype(held_as)


def setup_inputs(seed: int = 0) -> dict:
    splits = jax.random.split(jax.random.key(seed), 7)
    return {
        "queries": draw_queries(jax.random.fold_in(splits[6], 71), 0),
        "keys": draw_keys(jax.random.fold_in(splits[6], 71), 0),
        "values": centred(splits[2], (TOKENS, HEADS, HDIM), 1.0, 5.0, ((0, 64), (1, 4))),
        "grad_out": centred(splits[3], (TOKENS, D), 1.0, 6.0, ((0, 64), (1, 4))),
        "w_out": centred(splits[4], (D, D), D ** -0.5, 0.109375, ((0, 4),)),
        "crit": draw_crit(jax.random.fold_in(splits[6], 71), 0),
    }


def reference(queries, keys, values, grad_out, w_out, crit):
    d_attn = jnp.dot(grad_out, w_out.T, preferred_element_type=jnp.float32).astype(jnp.bfloat16)
    d_attn = d_attn.reshape(TOKENS, HEADS, HDIM)
    blocks = TOKENS // TOK_DEV
    scale = HDIM ** -0.5
    tile_off = jnp.arange(KT, dtype=jnp.int32)

    def step(carry, b):
        acc_k, acc_v = carry
        start = b * TOK_DEV
        own_idx = start + jnp.arange(TOK_DEV, dtype=jnp.int32)
        left_idx = start - KT + tile_off
        right_idx = start + TOK_DEV + tile_off
        tiles = lax.dynamic_index_in_dim(crit, b, 0, keepdims=False)
        far_idx = (tiles[:, None] * KT + tile_off[None, :]).reshape(-1)
        index = jnp.concatenate([left_idx, own_idx, right_idx, far_idx]).astype(jnp.int32)
        valid = jnp.concatenate([jnp.broadcast_to(b > 0, (KT,)), jnp.ones((TOK_DEV,), bool),
                                 jnp.broadcast_to(b < blocks - 1, (KT,)), jnp.repeat(tiles >= 0, KT)])
        safe = jnp.clip(index, 0, TOKENS - 1).astype(jnp.int32)
        query = lax.dynamic_slice_in_dim(queries, start, TOK_DEV, 0).astype(jnp.float32)
        grad_o = lax.dynamic_slice_in_dim(d_attn, start, TOK_DEV, 0).astype(jnp.float32)
        key_b = jnp.take(keys, safe, axis=0).astype(jnp.float32)
        val_b = jnp.take(values, safe, axis=0).astype(jnp.float32)
        scores = jnp.einsum("qhd,khd->hqk", query, key_b) * scale
        scores = jnp.where(valid[None, None, :], scores, -1e30)
        top = jnp.max(scores, axis=-1, keepdims=True)
        probs = jnp.exp(scores - top)
        probs = probs / jnp.sum(probs, axis=-1, keepdims=True)
        probs_b = probs.astype(jnp.bfloat16)
        dprob = jnp.einsum("qhd,khd->hqk", grad_o, val_b)
        delta = jnp.sum(probs * dprob, axis=-1, keepdims=True)
        dscore = (probs * (dprob - delta) * scale).astype(jnp.bfloat16)
        grad_q = jnp.einsum("hqk,khd->qhd", dscore.astype(jnp.float32), key_b).astype(jnp.bfloat16)
        weight = valid.astype(jnp.float32)[:, None, None]
        part_k = jnp.einsum("hqk,qhd->khd", dscore.astype(jnp.float32), query) * weight
        part_v = jnp.einsum("hqk,qhd->khd", probs_b.astype(jnp.float32), grad_o) * weight
        acc_k = acc_k.at[safe].add(part_k)
        acc_v = acc_v.at[safe].add(part_v)
        return (acc_k, acc_v), grad_q

    zeros = jnp.zeros((TOKENS, HEADS, HDIM), jnp.float32)
    (acc_k, acc_v), grad_qs = lax.scan(step, (zeros, zeros), jnp.arange(blocks, dtype=jnp.int32))
    return grad_qs.reshape(TOKENS, HEADS, HDIM), acc_k.astype(jnp.bfloat16), acc_v.astype(jnp.bfloat16)
```

```python
import functools
import math

import jax
import jax.numpy as jnp
from jax import lax
from jax.experimental import pallas as pl
from jax.experimental.pallas import tpu as pltpu
from jax.sharding import Mesh
from jax.sharding import PartitionSpec as P

KT = 16
HD = 128
TOK = ("x_lo", "z", "y")
PLANE = ("x_lo", "y")
HEAD = ("x_hi", "core")
VMEM_LIMIT = 48 * 1024 * 1024
PARTS = ((0, 3, False), (3, 6, False))


def serve_kernel(asked_ref, pair_ref, out_ref):
    step = pl.program_id(0)
    block, sources = out_ref.shape[0], pair_ref.shape[0]
    for i in range(block):
        tile = jnp.maximum(asked_ref[step * block + i], 0)
        rows = pl.ds(pl.multiple_of(tile * KT, KT), KT)
        for kind in range(2):
            out_ref[i, kind] = pair_ref[i % sources, kind, rows, :]


def serve(asked, pair, block):
    count = asked.shape[0]
    width = pair.shape[-1]
    return pl.pallas_call(
        serve_kernel,
        out_shape=jax.ShapeDtypeStruct((count, 2, KT, width), pair.dtype),
        grid_spec=pltpu.PrefetchScalarGridSpec(
            num_scalar_prefetch=1,
            grid=(count // block,),
            in_specs=[pl.BlockSpec(pair.shape, lambda i, a: (0, 0, 0, 0))],
            out_specs=pl.BlockSpec((block, 2, KT, width), lambda i, a: (i, 0, 0, 0)),
        ),
        compiler_params=pltpu.CompilerParams(vmem_limit_bytes=VMEM_LIMIT),
    )(asked, pair)


def attend_kernel(
    tiles, src_ref, dst_ref, num_ref, q_ref, do_ref, kv_ref, far_ref, dq_ref, own_ref, out_ref, k_all, v_all
):
    rows = q_ref.shape[0]
    total = rows + tiles * KT
    scale = HD**-0.5
    k_all[:rows] = kv_ref[0]
    v_all[:rows] = kv_ref[1]
    for j in range(tiles):
        slot = src_ref[j]
        at = rows + j * KT
        k_all[at : at + KT] = far_ref[slot, 0]
        v_all[at : at + KT] = far_ref[slot, 1]
    q = q_ref[...]
    do = do_ref[...]
    scores = lax.dot_general(
        k_all[...], q, (((1,), (1,)), ((), ())), preferred_element_type=jnp.float32
    )
    row = lax.broadcasted_iota(jnp.int32, (total, rows), 0)
    scores = jnp.where(row < rows + num_ref[0] * KT, scores, -1e30)
    top = jnp.max(scores, axis=0, keepdims=True)
    weight = jnp.exp2((scores - top) * (scale * math.log2(math.e)))
    probs = weight * (1.0 / jnp.sum(weight, axis=0, keepdims=True))
    dprob = lax.dot_general(
        v_all[...], do, (((1,), (1,)), ((), ())), preferred_element_type=jnp.float32
    )
    delta = jnp.sum(probs * dprob, axis=0, keepdims=True)
    dscore = (probs * (dprob - delta) * scale).astype(jnp.bfloat16)
    probs_b = probs.astype(jnp.bfloat16)
    dq_ref[...] = lax.dot_general(
        dscore, k_all[...], (((0,), (0,)), ((), ())), preferred_element_type=jnp.float32
    ).astype(jnp.bfloat16)
    for kind, (left, right) in enumerate(((dscore, q), (probs_b, do))):
        part = jnp.dot(left, right, preferred_element_type=jnp.float32)
        own_ref[kind] = part[:rows]
        far = part[rows:].astype(jnp.bfloat16)
        for j in range(tiles):
            out_ref[dst_ref[j], kind] = far[j * KT : (j + 1) * KT]


def attend(src, dst, num, q, do, kv, far, first, heads):
    rows = q.shape[0]
    tiles = src.shape[0]
    slots = far.shape[0]
    total = rows + tiles * KT
    whole = lambda h, *_: (0, first + h)
    return pl.pallas_call(
        functools.partial(attend_kernel, tiles),
        out_shape=(
            jax.ShapeDtypeStruct((rows, heads * HD), jnp.bfloat16),
            jax.ShapeDtypeStruct((2, rows, heads * HD), jnp.float32),
            jax.ShapeDtypeStruct((slots, 2, KT, heads * HD), jnp.bfloat16),
        ),
        grid_spec=pltpu.PrefetchScalarGridSpec(
            num_scalar_prefetch=3,
            grid=(heads,),
            in_specs=[
                pl.BlockSpec((rows, HD), whole),
                pl.BlockSpec((rows, HD), whole),
                pl.BlockSpec((2, rows, HD), lambda h, *_: (0, 0, first + h)),
                pl.BlockSpec((slots, 2, KT, HD), lambda h, *_: (0, 0, 0, h)),
            ],
            out_specs=(
                pl.BlockSpec((rows, HD), lambda h, *_: (0, h)),
                pl.BlockSpec((2, rows, HD), lambda h, *_: (0, 0, h)),
                pl.BlockSpec((slots, 2, KT, HD), lambda h, *_: (0, 0, 0, h)),
            ),
            scratch_shapes=[
                pltpu.VMEM((total, HD), jnp.bfloat16),
                pltpu.VMEM((total, HD), jnp.bfloat16),
            ],
        ),
        compiler_params=pltpu.CompilerParams(vmem_limit_bytes=VMEM_LIMIT),
    )(src, dst, num, q, do, kv, far)


def settle_kernel(asked_ref, own_ref, back_ref, out_ref, acc):
    rows = own_ref.shape[1]
    acc[:, :rows] = own_ref[...]
    for s in range(back_ref.shape[0]):
        asked = asked_ref[s]
        tile = jnp.where(asked >= 0, asked, rows // KT)
        at = pl.ds(pl.multiple_of(tile * KT, KT), KT)
        for kind in range(2):
            acc[kind, at] += back_ref[s, kind].astype(jnp.float32)
    out_ref[...] = acc[:, :rows].astype(jnp.bfloat16)


def settle(asked, own, back):
    _, rows, width = own.shape
    slots = back.shape[0]
    return pl.pallas_call(
        settle_kernel,
        out_shape=jax.ShapeDtypeStruct((2, rows, width), jnp.bfloat16),
        grid_spec=pltpu.PrefetchScalarGridSpec(
            num_scalar_prefetch=1,
            grid=(width // HD,),
            in_specs=[
                pl.BlockSpec((2, rows, HD), lambda h, *_: (0, 0, h)),
                pl.BlockSpec((slots, 2, KT, HD), lambda h, *_: (0, 0, 0, h)),
            ],
            out_specs=pl.BlockSpec((2, rows, HD), lambda h, *_: (0, 0, h)),
            scratch_shapes=[pltpu.VMEM((2, rows + KT, HD), jnp.float32)],
        ),
        compiler_params=pltpu.CompilerParams(vmem_limit_bytes=VMEM_LIMIT),
    )(asked, own, back)


def shards(queries, keys, values, grad_out, w_out, crit):
    rows, heads, _ = queries.shape
    tiles_here = rows // KT
    sizes = tuple(lax.axis_size(a) for a in TOK)
    nx, nz, ny = sizes
    count = nx * nz * ny
    place = lax.axis_index(TOK)
    z = lax.axis_index("z")
    entries = jnp.concatenate([crit[0], jnp.stack([place * tiles_here - 1, (place + 1) * tiles_here])])
    used = (entries >= 0) & (entries < count * tiles_here)
    owner = jnp.where(used, entries // tiles_here, place)
    blocks = jnp.arange(count)
    want = jnp.max(
        jnp.where(used[None, :] & (owner[None, :] == blocks[:, None]), entries[None, :] % tiles_here, -1), axis=1
    )
    told = jnp.broadcast_to(
        want.reshape(nx, 1, nz, ny).transpose(0, 1, 3, 2), (nx, nz, ny, nz)
    ).reshape(count, nz)
    heard = lax.all_to_all(told, TOK, 0, 0, tiled=True)
    asked = lax.dynamic_index_in_dim(heard, z, 1, keepdims=False)

    pair = jnp.stack([keys.reshape(rows, heads * HD), values.reshape(rows, heads * HD)])
    far = []
    for first, last, _ in PARTS:
        part = pair[:, :, first * HD : last * HD][None]
        far.append(lax.all_to_all(serve(asked, part, 8), TOK, 0, 0, tiled=True))

    d_attn = lax.dot_general(
        lax.all_gather(grad_out, HEAD, axis=1, tiled=True),
        w_out,
        (((1,), (1,)), ((), ())),
        preferred_element_type=jnp.float32,
    ).astype(jnp.bfloat16)
    flat_q = queries.reshape(rows, heads * HD)

    tiles = entries.shape[0]
    order = jnp.arange(tiles)
    rank = jnp.sum(used[None, :] & (order[None, :] < order[:, None]), axis=1)
    slot_of = jnp.max(
        jnp.where(used[None, :] & (rank[None, :] == order[:, None]), owner[None, :], -1), axis=1
    ).astype(jnp.int32)
    slot_of = jnp.where(slot_of >= 0, slot_of, place).astype(jnp.int32)
    number = jnp.sum(used.astype(jnp.int32)).reshape(1)

    grad_q, totals = [], []
    for (first, last, _), got in zip(PARTS, far):
        dq, own, out = attend(slot_of, slot_of, number, flat_q, d_attn, pair, got, first, last - first)
        back = lax.all_to_all(out, TOK, 0, 0, tiled=True)
        grad_q.append(dq)
        totals.append(settle(asked, own, back))
    grad_q = jnp.concatenate(grad_q, axis=1).reshape(rows, heads, HD)
    totals = jnp.concatenate(totals, axis=2).reshape(2, rows, heads, HD)
    return grad_q, totals[0], totals[1]


def solution(mesh):
    fine = Mesh(mesh.devices.reshape(2, 8, 4, 2, 2), TOK + HEAD)
    return jax.shard_map(
        shards,
        mesh=fine,
        in_specs=(
            P(TOK, HEAD, None),
            P(TOK, HEAD, None),
            P(TOK, HEAD, None),
            P(TOK, HEAD),
            P(HEAD, None),
            P(TOK, None),
        ),
        out_specs=(P(TOK, HEAD, None), P(TOK, HEAD, None), P(TOK, HEAD, None)),
        check_vma=False,
    )
```

```python
import functools
import math

import jax
import jax.numpy as jnp
from jax import lax
from jax.experimental import pallas as pl
from jax.experimental.pallas import tpu as pltpu
from jax.sharding import Mesh
from jax.sharding import PartitionSpec as P

KT = 16
HD = 128
TOK = ("x_lo", "z", "y")
PLANE = ("x_lo", "y")
HEAD = ("x_hi", "core")
VMEM_LIMIT = 48 * 1024 * 1024
PARTS = ((0, 3, False), (3, 6, False))


def serve_kernel(asked_ref, pair_ref, out_ref):
    step = pl.program_id(0)
    block, sources = out_ref.shape[0], pair_ref.shape[0]
    for i in range(block):
        tile = jnp.maximum(asked_ref[step * block + i], 0)
        rows = pl.ds(pl.multiple_of(tile * KT, KT), KT)
        for kind in range(2):
            out_ref[i, kind] = pair_ref[i % sources, kind, rows, :]


def serve(asked, pair, block):
    count = asked.shape[0]
    width = pair.shape[-1]
    return pl.pallas_call(
        serve_kernel,
        out_shape=jax.ShapeDtypeStruct((count, 2, KT, width), pair.dtype),
        grid_spec=pltpu.PrefetchScalarGridSpec(
            num_scalar_prefetch=1,
            grid=(count // block,),
            in_specs=[pl.BlockSpec(pair.shape, lambda i, a: (0, 0, 0, 0))],
            out_specs=pl.BlockSpec((block, 2, KT, width), lambda i, a: (i, 0, 0, 0)),
        ),
        compiler_params=pltpu.CompilerParams(vmem_limit_bytes=VMEM_LIMIT),
    )(asked, pair)


def attend_kernel(
    tiles, src_ref, dst_ref, num_ref, q_ref, do_ref, kv_ref, far_ref, dq_ref, own_ref, out_ref, k_all, v_all
):
    rows = q_ref.shape[0]
    total = rows + tiles * KT
    scale = HD**-0.5
    k_all[:rows] = kv_ref[0]
    v_all[:rows] = kv_ref[1]
    for j in range(tiles):
        slot = src_ref[j]
        at = rows + j * KT
        k_all[at : at + KT] = far_ref[slot, 0]
        v_all[at : at + KT] = far_ref[slot, 1]
    q = q_ref[...]
    do = do_ref[...]
    scores = lax.dot_general(
        k_all[...], q, (((1,), (1,)), ((), ())), preferred_element_type=jnp.float32
    )
    row = lax.broadcasted_iota(jnp.int32, (total, rows), 0)
    scores = jnp.where(row < rows + num_ref[0] * KT, scores, -1e30)
    top = jnp.max(scores, axis=0, keepdims=True)
    weight = jnp.exp2((scores - top) * (scale * math.log2(math.e)))
    probs = weight * (1.0 / jnp.sum(weight, axis=0, keepdims=True))
    dprob = lax.dot_general(
        v_all[...], do, (((1,), (1,)), ((), ())), preferred_element_type=jnp.float32
    )
    delta = jnp.sum(probs * dprob, axis=0, keepdims=True)
    dscore = (probs * (dprob - delta) * scale).astype(jnp.bfloat16)
    probs_b = probs.astype(jnp.bfloat16)
    dq_ref[...] = lax.dot_general(
        dscore, k_all[...], (((0,), (0,)), ((), ())), preferred_element_type=jnp.float32
    ).astype(jnp.bfloat16)
    for kind, (left, right) in enumerate(((dscore, q), (probs_b, do))):
        part = jnp.dot(left, right, preferred_element_type=jnp.float32)
        own_ref[kind] = part[:rows]
        far = part[rows:].astype(jnp.bfloat16)
        for j in range(tiles):
            out_ref[dst_ref[j], kind] = far[j * KT : (j + 1) * KT]


def attend(src, dst, num, q, do, kv, far, first, heads):
    rows = q.shape[0]
    tiles = src.shape[0]
    slots = far.shape[0]
    total = rows + tiles * KT
    whole = lambda h, *_: (0, first + h)
    return pl.pallas_call(
        functools.partial(attend_kernel, tiles),
        out_shape=(
            jax.ShapeDtypeStruct((rows, heads * HD), jnp.bfloat16),
            jax.ShapeDtypeStruct((2, rows, heads * HD), jnp.float32),
            jax.ShapeDtypeStruct((slots, 2, KT, heads * HD), jnp.bfloat16),
        ),
        grid_spec=pltpu.PrefetchScalarGridSpec(
            num_scalar_prefetch=3,
            grid=(heads,),
            in_specs=[
                pl.BlockSpec((rows, HD), whole),
                pl.BlockSpec((rows, HD), whole),
                pl.BlockSpec((2, rows, HD), lambda h, *_: (0, 0, first + h)),
                pl.BlockSpec((slots, 2, KT, HD), lambda h, *_: (0, 0, 0, h)),
            ],
            out_specs=(
                pl.BlockSpec((rows, HD), lambda h, *_: (0, h)),
                pl.BlockSpec((2, rows, HD), lambda h, *_: (0, 0, h)),
                pl.BlockSpec((slots, 2, KT, HD), lambda h, *_: (0, 0, 0, h)),
            ),
            scratch_shapes=[
                pltpu.VMEM((total, HD), jnp.bfloat16),
                pltpu.VMEM((total, HD), jnp.bfloat16),
            ],
        ),
        compiler_params=pltpu.CompilerParams(vmem_limit_bytes=VMEM_LIMIT),
    )(src, dst, num, q, do, kv, far)


def settle_kernel(asked_ref, own_ref, back_ref, out_ref, acc):
    rows = own_ref.shape[1]
    acc[:, :rows] = own_ref[...]
    for s in range(back_ref.shape[0]):
        asked = asked_ref[s]
        tile = jnp.where(asked >= 0, asked, rows // KT)
        at = pl.ds(pl.multiple_of(tile * KT, KT), KT)
        for kind in range(2):
            acc[kind, at] += back_ref[s, kind].astype(jnp.float32)
    out_ref[...] = acc[:, :rows].astype(jnp.bfloat16)


def settle(asked, own, back):
    _, rows, width = own.shape
    slots = back.shape[0]
    return pl.pallas_call(
        settle_kernel,
        out_shape=jax.ShapeDtypeStruct((2, rows, width), jnp.bfloat16),
        grid_spec=pltpu.PrefetchScalarGridSpec(
            num_scalar_prefetch=1,
            grid=(width // HD,),
            in_specs=[
                pl.BlockSpec((2, rows, HD), lambda h, *_: (0, 0, h)),
                pl.BlockSpec((slots, 2, KT, HD), lambda h, *_: (0, 0, 0, h)),
            ],
            out_specs=pl.BlockSpec((2, rows, HD), lambda h, *_: (0, 0, h)),
            scratch_shapes=[pltpu.VMEM((2, rows + KT, HD), jnp.float32)],
        ),
        compiler_params=pltpu.CompilerParams(vmem_limit_bytes=VMEM_LIMIT),
    )(asked, own, back)


def project_kernel(me_ref, own_ref, flip_ref, both_ref, w_ref, out_ref, acc):
    step = pl.program_id(0)

    def add(rows):
        part = lax.dot_general(rows, w_ref[...], (((1,), (1,)), ((), ())), preferred_element_type=jnp.float32)
        acc[...] = jnp.where(step == 0, part, acc[...] + part)

    @pl.when(step == 0)
    def _():
        add(own_ref[...])

    @pl.when(step == 1)
    def _():
        add(flip_ref[...])

    @pl.when(step == 2)
    def _():
        add(both_ref[0])

    @pl.when(step == 3)
    def _():
        add(both_ref[1])
        out_ref[...] = acc[...].astype(out_ref.dtype)


def project(grad_out, w_out):
    rows, width = grad_out.shape
    out_width = w_out.shape[0]
    swap = [(0, 1), (1, 0)]
    flip = lax.ppermute(grad_out, HEAD[0], swap)
    both = lax.ppermute(jnp.stack([grad_out, flip]), HEAD[1], swap)
    me = (lax.axis_index(HEAD[0]) * 2 + lax.axis_index(HEAD[1])).astype(jnp.int32).reshape(1)
    block = lambda i, m: (0, m[0] ^ (i // 2 + (i % 2) * 2))
    return pl.pallas_call(
        project_kernel,
        out_shape=jax.ShapeDtypeStruct((rows, out_width), jnp.bfloat16),
        grid_spec=pltpu.PrefetchScalarGridSpec(
            num_scalar_prefetch=1,
            grid=(4,),
            in_specs=[
                pl.BlockSpec((rows, width), lambda i, m: (0, 0)),
                pl.BlockSpec((rows, width), lambda i, m: (0, 0)),
                pl.BlockSpec((2, rows, width), lambda i, m: (0, 0, 0)),
                pl.BlockSpec((out_width, width), block),
            ],
            out_specs=pl.BlockSpec((rows, out_width), lambda i, m: (0, 0)),
            scratch_shapes=[pltpu.VMEM((rows, out_width), jnp.float32)],
        ),
        compiler_params=pltpu.CompilerParams(vmem_limit_bytes=VMEM_LIMIT),
    )(me, grad_out, flip, both, w_out)


def shards(queries, keys, values, grad_out, w_out, crit):
    rows, heads, _ = queries.shape
    tiles_here = rows // KT
    sizes = tuple(lax.axis_size(a) for a in TOK)
    nx, nz, ny = sizes
    count = nx * nz * ny
    place = lax.axis_index(TOK)
    z = lax.axis_index("z")
    entries = jnp.concatenate([crit[0], jnp.stack([place * tiles_here - 1, (place + 1) * tiles_here])])
    used = (entries >= 0) & (entries < count * tiles_here)
    owner = jnp.where(used, entries // tiles_here, place)
    blocks = jnp.arange(count)
    want = jnp.max(
        jnp.where(used[None, :] & (owner[None, :] == blocks[:, None]), entries[None, :] % tiles_here, -1), axis=1
    )
    told = jnp.broadcast_to(
        want.reshape(nx, 1, nz, ny).transpose(0, 1, 3, 2), (nx, nz, ny, nz)
    ).reshape(count, nz)
    heard = lax.all_to_all(told, TOK, 0, 0, tiled=True)
    asked = lax.dynamic_index_in_dim(heard, z, 1, keepdims=False)

    pair = jnp.stack([keys.reshape(rows, heads * HD), values.reshape(rows, heads * HD)])
    far = []
    for first, last, _ in PARTS:
        part = pair[:, :, first * HD : last * HD][None]
        far.append(lax.all_to_all(serve(asked, part, 8), TOK, 0, 0, tiled=True))

    d_attn = project(grad_out, w_out)
    flat_q = queries.reshape(rows, heads * HD)

    tiles = entries.shape[0]
    order = jnp.arange(tiles)
    rank = jnp.sum(used[None, :] & (order[None, :] < order[:, None]), axis=1)
    slot_of = jnp.max(
        jnp.where(used[None, :] & (rank[None, :] == order[:, None]), owner[None, :], -1), axis=1
    ).astype(jnp.int32)
    slot_of = jnp.where(slot_of >= 0, slot_of, place).astype(jnp.int32)
    number = jnp.sum(used.astype(jnp.int32)).reshape(1)

    grad_q, totals = [], []
    for (first, last, _), got in zip(PARTS, far):
        dq, own, out = attend(slot_of, slot_of, number, flat_q, d_attn, pair, got, first, last - first)
        back = lax.all_to_all(out, TOK, 0, 0, tiled=True)
        grad_q.append(dq)
        totals.append(settle(asked, own, back))
    grad_q = jnp.concatenate(grad_q, axis=1).reshape(rows, heads, HD)
    totals = jnp.concatenate(totals, axis=2).reshape(2, rows, heads, HD)
    return grad_q, totals[0], totals[1]


def solution(mesh):
    fine = Mesh(mesh.devices.reshape(2, 8, 4, 2, 2), TOK + HEAD)
    return jax.shard_map(
        shards,
        mesh=fine,
        in_specs=(
            P(TOK, HEAD, None),
            P(TOK, HEAD, None),
            P(TOK, HEAD, None),
            P(TOK, HEAD),
            P(HEAD, None),
            P(TOK, None),
        ),
        out_specs=(P(TOK, HEAD, None), P(TOK, HEAD, None), P(TOK, HEAD, None)),
        check_vma=False,
    )
```

```python
import functools
import math

import jax
import jax.numpy as jnp
from jax import lax
from jax.experimental import pallas as pl
from jax.experimental.pallas import tpu as pltpu
from jax.sharding import Mesh
from jax.sharding import PartitionSpec as P

KT = 16
HD = 128
TOK = ("x_lo", "z", "y")
PLANE = ("x_lo", "y")
HEAD = ("x_hi", "core")
VMEM_LIMIT = 48 * 1024 * 1024
RING = 3
STEPS = (0, -1, 1, -2, 2, -3, 3, 4)
PARAMS = pltpu.CompilerParams(vmem_limit_bytes=VMEM_LIMIT)
VMEM = pl.BlockSpec(memory_space=pltpu.VMEM)
SMEM = pl.BlockSpec(memory_space=pltpu.SMEM)


def tile_rows(tile):
    return pl.ds(pl.multiple_of(tile * KT, KT), KT)


def serve_all_kernel(first, asked_ref, k_ref, v_ref, out_ref):
    block, heads = out_ref.shape[:2]
    for i in range(block):
        rows = tile_rows(jnp.maximum(asked_ref[pl.program_id(0) * block + i], 0))
        for h in range(heads):
            out_ref[i, h, 0] = k_ref[first + h, rows, :]
            out_ref[i, h, 1] = v_ref[first + h, rows, :]


def serve_all(asked, keys, values, first, block=16):
    count, heads = asked.shape[0], keys.shape[0] - first
    whole = pl.BlockSpec(keys.shape, lambda i, a: (0, 0, 0))
    return pl.pallas_call(
        functools.partial(serve_all_kernel, first),
        out_shape=jax.ShapeDtypeStruct((count, heads, 2, KT, HD), keys.dtype),
        grid_spec=pltpu.PrefetchScalarGridSpec(
            num_scalar_prefetch=1,
            grid=(count // block,),
            in_specs=[whole, whole],
            out_specs=pl.BlockSpec((block, heads, 2, KT, HD), lambda i, a: (i, 0, 0, 0, 0)),
        ),
        compiler_params=PARAMS,
    )(asked, keys, values)


def serve_plane_kernel(sizes, wanted_ref, pos_ref, *refs):
    nx, nz, ny = sizes
    held, outs = refs[: len(STEPS) + 1], refs[len(STEPS) + 1 :]
    heads = outs[0].shape[1]
    for r in range(nx * ny):
        mate = lax.rem(pos_ref[0] + r // ny, nx) * ny + lax.rem(pos_ref[2] + r % ny, ny)
        for s, step in enumerate(STEPS):
            tile = wanted_ref[mate * nz + lax.rem(pos_ref[1] + step + nz, nz)]
            rows = tile_rows(jnp.maximum(tile, 0))
            for h in range(heads):
                for kind in range(2):
                    if s < len(STEPS) - 1:
                        outs[r][s, h, kind] = held[s][kind, h, rows, :]
                    else:
                        outs[r][s, h, kind] = held[s + kind][h, rows, :]


def serve_plane(sizes, wanted, pos, held):
    mates = sizes[0] * sizes[2]
    heads = held[0].shape[1]
    return pl.pallas_call(
        functools.partial(serve_plane_kernel, sizes),
        out_shape=[jax.ShapeDtypeStruct((len(STEPS), heads, 2, KT, HD), held[0].dtype)] * mates,
        in_specs=[SMEM] * 2 + [VMEM] * len(held),
        out_specs=[VMEM] * mates,
        compiler_params=PARAMS,
    )(wanted, pos, *held)


def attend_kernel(tiles, parts, src_ref, dst_ref, num_ref, q_ref, do_ref, k_ref, v_ref, *refs):
    fars, (dq_ref, own_ref, out_ref, k_all, v_all) = refs[:parts], refs[-5 - (parts > 1) :][:5]
    rows = q_ref.shape[1]
    total = rows + tiles * KT
    scale = HD**-0.5
    if parts > 1:
        far_ref = refs[-1]
        each = fars[0].shape[0]
        for i in range(parts):
            far_ref[i * each : (i + 1) * each] = fars[i][:, 0]
        load = lambda slot, kind: far_ref[slot, kind]
    else:
        load = lambda slot, kind: fars[0][slot, 0, kind]
    k_all[:rows] = k_ref[0]
    v_all[:rows] = v_ref[0]
    for j in range(tiles):
        slot = src_ref[j]
        at = rows + j * KT
        k_all[at : at + KT] = load(slot, 0)
        v_all[at : at + KT] = load(slot, 1)
    q = q_ref[0]
    do = do_ref[...]
    scores = lax.dot_general(
        k_all[...], q, (((1,), (1,)), ((), ())), preferred_element_type=jnp.float32
    )
    row = lax.broadcasted_iota(jnp.int32, (total, rows), 0)
    scores = jnp.where(row < rows + num_ref[0] * KT, scores, -1e30)
    top = jnp.max(scores, axis=0, keepdims=True)
    weight = jnp.exp2((scores - top) * (scale * math.log2(math.e)))
    probs = weight * (1.0 / jnp.sum(weight, axis=0, keepdims=True))
    dprob = lax.dot_general(
        v_all[...], do, (((1,), (1,)), ((), ())), preferred_element_type=jnp.float32
    )
    delta = jnp.sum(probs * dprob, axis=0, keepdims=True)
    dscore = (probs * (dprob - delta) * scale).astype(jnp.bfloat16)
    probs_b = probs.astype(jnp.bfloat16)
    dq_ref[0] = lax.dot_general(
        dscore, k_all[...], (((0,), (0,)), ((), ())), preferred_element_type=jnp.float32
    ).astype(jnp.bfloat16)
    for kind, (left, right) in enumerate(((dscore, q), (probs_b, do))):
        part = jnp.dot(left, right, preferred_element_type=jnp.float32)
        own_ref[kind, 0] = part[:rows]
        far = part[rows:].astype(jnp.bfloat16)
        for j in range(tiles):
            out_ref[dst_ref[j], 0, kind] = far[j * KT : (j + 1) * KT]


def attend(src, dst, num, q, do, keys, values, fars, first, earlier=()):
    heads, rows, _ = q.shape
    tiles = src.shape[0]
    parts = len(fars)
    each, here = fars[0].shape[:2]
    slots = parts * each
    total = rows + tiles * KT
    own = pl.BlockSpec((1, rows, HD), lambda h, *_: (first + h, 0, 0))
    return pl.pallas_call(
        functools.partial(attend_kernel, tiles, parts),
        out_shape=(
            jax.ShapeDtypeStruct((heads, rows, HD), jnp.bfloat16),
            jax.ShapeDtypeStruct((2, heads, rows, HD), jnp.float32),
            jax.ShapeDtypeStruct((slots, heads, 2, KT, HD), jnp.bfloat16),
        ),
        grid_spec=pltpu.PrefetchScalarGridSpec(
            num_scalar_prefetch=3,
            grid=(here,),
            in_specs=[own, pl.BlockSpec((rows, HD), lambda h, *_: (0, first + h)), own, own]
            + [pl.BlockSpec((each, 1, 2, KT, HD), lambda h, *_: (0, h, 0, 0, 0))] * parts
            + [pl.BlockSpec(memory_space=pl.ANY)] * len(earlier),
            out_specs=(
                own,
                pl.BlockSpec((2, 1, rows, HD), lambda h, *_: (0, first + h, 0, 0)),
                pl.BlockSpec((slots, 1, 2, KT, HD), lambda h, *_: (0, first + h, 0, 0, 0)),
            ),
            scratch_shapes=[
                pltpu.VMEM((total, HD), jnp.bfloat16),
                pltpu.VMEM((total, HD), jnp.bfloat16),
            ]
            + ([pltpu.VMEM((slots, 2, KT, HD), jnp.bfloat16)] if parts > 1 else []),
        ),
        input_output_aliases={7 + parts + i: i for i in range(len(earlier))},
        compiler_params=PARAMS,
    )(src, dst, num, q, do, keys, values, *fars, *earlier)


def settle_kernel(asked_ref, own_ref, back_ref, dk_ref, dv_ref, *accs):
    slots, heads = back_ref.shape[:2]
    rows = own_ref.shape[2]
    for h in range(heads):
        for kind in range(2):
            accs[h * 2 + kind][:rows] = own_ref[kind, h]
    for s in range(slots):
        asked = asked_ref[s]
        at = tile_rows(jnp.where(asked >= 0, asked, rows // KT))
        for h in range(heads):
            for kind in range(2):
                accs[h * 2 + kind][at] += back_ref[s, h, kind].astype(jnp.float32)
    for h in range(heads):
        for kind, out in enumerate((dk_ref, dv_ref)):
            out[h] = accs[h * 2 + kind][:rows].astype(jnp.bfloat16)


def settle(asked, own, back, block=2):
    _, heads, rows, _ = own.shape
    slots = back.shape[0]
    out = pl.BlockSpec((block, rows, HD), lambda h, *_: (h, 0, 0))
    return pl.pallas_call(
        settle_kernel,
        out_shape=[jax.ShapeDtypeStruct((heads, rows, HD), jnp.bfloat16)] * 2,
        grid_spec=pltpu.PrefetchScalarGridSpec(
            num_scalar_prefetch=1,
            grid=(heads // block,),
            in_specs=[
                pl.BlockSpec((2, block, rows, HD), lambda h, *_: (0, h, 0, 0)),
                pl.BlockSpec((slots, block, 2, KT, HD), lambda h, *_: (0, h, 0, 0, 0)),
            ],
            out_specs=[out, out],
            scratch_shapes=[pltpu.VMEM((rows + KT, HD), jnp.float32)] * (2 * block),
        ),
        compiler_params=PARAMS,
    )(asked, own, back)


def project_kernel(me_ref, own_ref, flip_ref, both_ref, w_ref, out_ref, acc):
    step = pl.program_id(0)

    def add(rows):
        part = lax.dot_general(rows, w_ref[...], (((1,), (1,)), ((), ())), preferred_element_type=jnp.float32)
        acc[...] = jnp.where(step == 0, part, acc[...] + part)

    @pl.when(step == 0)
    def _():
        add(own_ref[...])

    @pl.when(step == 1)
    def _():
        add(flip_ref[...])

    @pl.when(step == 2)
    def _():
        add(both_ref[0])

    @pl.when(step == 3)
    def _():
        add(both_ref[1])
        out_ref[...] = acc[...].astype(out_ref.dtype)


def columns(grad_out):
    swap = [(0, 1), (1, 0)]
    flip = lax.ppermute(grad_out, HEAD[0], swap)
    return flip, lax.ppermute(jnp.stack([grad_out, flip]), HEAD[1], swap)


def project(grad_out, flip, both, w_out):
    rows, width = grad_out.shape
    out_width = w_out.shape[0]
    me = (lax.axis_index(HEAD[0]) * 2 + lax.axis_index(HEAD[1])).astype(jnp.int32).reshape(1)
    block = lambda i, m: (0, m[0] ^ (i // 2 + (i % 2) * 2))
    return pl.pallas_call(
        project_kernel,
        out_shape=jax.ShapeDtypeStruct((rows, out_width), jnp.bfloat16),
        grid_spec=pltpu.PrefetchScalarGridSpec(
            num_scalar_prefetch=1,
            grid=(4,),
            in_specs=[
                pl.BlockSpec((rows, width), lambda i, m: (0, 0)),
                pl.BlockSpec((rows, width), lambda i, m: (0, 0)),
                pl.BlockSpec((2, rows, width), lambda i, m: (0, 0, 0)),
                pl.BlockSpec((out_width, width), block),
            ],
            out_specs=pl.BlockSpec((rows, out_width), lambda i, m: (0, 0)),
            scratch_shapes=[pltpu.VMEM((rows, out_width), jnp.float32)],
        ),
        compiler_params=pltpu.CompilerParams(vmem_limit_bytes=VMEM_LIMIT),
    )(me, grad_out, flip, both, w_out)


def along_z(value, step):
    count = lax.axis_size("z")
    return lax.ppermute(value, "z", [(i, (i + step) % count) for i in range(count)])


def across_plane(value, dx, dy):
    nx, ny = lax.axis_size("x_lo"), lax.axis_size("y")
    pairs = [(x * ny + y, (x + dx) % nx * ny + (y + dy) % ny) for x in range(nx) for y in range(ny)]
    return lax.ppermute(value, PLANE, pairs)


def shards(queries, keys, values, grad_out, w_out, crit):
    queries, keys, values = (a.transpose(1, 0, 2) for a in (queries, keys, values))
    heads, rows, _ = queries.shape
    tiles_here = rows // KT
    sizes = tuple(lax.axis_size(a) for a in TOK)
    nx, nz, ny = sizes
    count = nx * nz * ny
    x, z, y = (lax.axis_index(a).astype(jnp.int32) for a in TOK)
    pos = jnp.stack([x, z, y])
    place = (x * nz + z) * ny + y

    entries = jnp.concatenate([crit[0], jnp.stack([place * tiles_here - 1, (place + 1) * tiles_here])])
    used = (entries >= 0) & (entries < count * tiles_here)
    owner = jnp.where(used, entries // tiles_here, place)
    blocks = jnp.arange(count)
    want = jnp.max(
        jnp.where(used[None, :] & (owner[None, :] == blocks[:, None]), entries[None, :] % tiles_here, -1), axis=1
    )
    wanted = lax.all_to_all(
        want.reshape(nx, nz, ny).transpose(0, 2, 1).reshape(nx * ny, nz), PLANE, 0, 0, tiled=True
    )
    asked = lax.all_to_all(wanted.T, "z", 0, 0, tiled=True)
    asked = asked.reshape(nz, nx, ny).transpose(1, 0, 2).reshape(count)
    wanted = wanted.reshape(nx * ny * nz)

    ring = jnp.stack([keys[:RING], values[:RING]])
    up, down = along_z(ring, 1), along_z(ring, -1)
    held = [ring, up, down]
    up, down, wanted = lax.optimization_barrier((up, down, wanted))
    up, down = along_z(up, 1), along_z(down, -1)
    held += [up, down]
    up, down, asked = lax.optimization_barrier((up, down, asked))
    up, down = along_z(up, 1), along_z(down, -1)
    held += [up, down]
    held += [along_z(up[0], 1), along_z(down[1], -1)]

    flip, both = columns(grad_out)

    tiles = entries.shape[0]
    order = jnp.arange(tiles)
    rank = jnp.sum(used[None, :] & (order[None, :] < order[:, None]), axis=1)
    slot = jnp.max(jnp.where(used[None, :] & (rank[None, :] == order[:, None]), owner[None, :], -1), axis=1)
    slot = jnp.where(slot >= 0, slot, place).astype(jnp.int32)
    number = jnp.sum(used.astype(jnp.int32)).reshape(1)
    dx, dz, dy = (x - slot // (nz * ny)) % nx, (slot // ny - z) % nz, (y - slot % ny) % ny
    rank_of = sum(jnp.where(dz == step % nz, s, 0) for s, step in enumerate(STEPS))
    plane_slot = ((dx * ny + dy) * len(STEPS) + rank_of).astype(jnp.int32)

    served = serve_all(asked, keys, values, RING)
    served, held, flip, both = lax.optimization_barrier((served, held, flip, both))
    far = lax.all_to_all(served, TOK, 0, 0, tiled=True)
    near = serve_plane(sizes, wanted, pos, held)
    near = [near[0]] + [across_plane(near[r], r // ny, r % ny) for r in range(1, nx * ny)]
    d_attn = project(grad_out, flip, both, w_out)

    done = attend(plane_slot, slot, number, queries, d_attn, keys, values, near, 0)
    grad_q, own, out = attend(slot, slot, number, queries, d_attn, keys, values, [far], RING, done)
    back = lax.all_to_all(out, TOK, 0, 0, tiled=True)
    grad_k, grad_v = settle(asked, own, back)
    return tuple(a.transpose(1, 0, 2) for a in (grad_q, grad_k, grad_v))


def solution(mesh):
    fine = Mesh(mesh.devices.reshape(2, 8, 4, 2, 2), TOK + HEAD)
    return jax.shard_map(
        shards,
        mesh=fine,
        in_specs=(
            P(TOK, HEAD, None),
            P(TOK, HEAD, None),
            P(TOK, HEAD, None),
            P(TOK, HEAD),
            P(HEAD, None),
            P(TOK, None),
        ),
        out_specs=(P(TOK, HEAD, None), P(TOK, HEAD, None), P(TOK, HEAD, None)),
        check_vma=False,
    )
```

```python
import functools
import math

import jax
import jax.numpy as jnp
from jax import lax
from jax.experimental import pallas as pl
from jax.experimental.pallas import tpu as pltpu
from jax.sharding import Mesh
from jax.sharding import PartitionSpec as P

KT = 16
HD = 128
TOK = ("x_lo", "z", "y")
PLANE = ("x_lo", "y")
HEAD = ("x_hi", "core")
MIB = 1024 * 1024
RING = 3
STEPS = (0, -1, 1, -2, 2, -3, 3, 4)
GROUP = 1
SMALL = pltpu.CompilerParams(vmem_limit_bytes=16 * MIB)
LARGE = pltpu.CompilerParams(vmem_limit_bytes=60 * MIB)


def tile_rows(tile):
    return pl.ds(pl.multiple_of(tile * KT, KT), KT)


def serve_all_kernel(first, asked_ref, k_ref, v_ref, out_ref):
    block, heads = out_ref.shape[:2]
    for i in range(block):
        rows = tile_rows(jnp.maximum(asked_ref[pl.program_id(0) * block + i], 0))
        for h in range(heads):
            out_ref[i, h, 0] = k_ref[first + h, rows, :]
            out_ref[i, h, 1] = v_ref[first + h, rows, :]


def serve_all(asked, keys, values, first, block=16):
    count, heads = asked.shape[0], keys.shape[0] - first
    whole = pl.BlockSpec(keys.shape, lambda i, a: (0, 0, 0))
    return pl.pallas_call(
        functools.partial(serve_all_kernel, first),
        out_shape=jax.ShapeDtypeStruct((count, heads, 2, KT, HD), keys.dtype),
        grid_spec=pltpu.PrefetchScalarGridSpec(
            num_scalar_prefetch=1,
            grid=(count // block,),
            in_specs=[whole, whole],
            out_specs=pl.BlockSpec((block, heads, 2, KT, HD), lambda i, a: (i, 0, 0, 0, 0)),
        ),
        compiler_params=SMALL,
    )(asked, keys, values)


def serve_plane_kernel(sizes, wanted_ref, pos_ref, *refs):
    nx, nz, ny = sizes
    held, outs = refs[: -nx * ny], refs[-nx * ny :]
    for r in range(nx * ny):
        mate = lax.rem(pos_ref[0] + r // ny, nx) * ny + lax.rem(pos_ref[2] + r % ny, ny)
        for s, step in enumerate(STEPS):
            tile = wanted_ref[mate * nz + lax.rem(pos_ref[1] + step + nz, nz)]
            rows = tile_rows(jnp.maximum(tile, 0))
            for kind in range(2):
                if s < len(STEPS) - 1:
                    outs[r][s, 0, kind] = held[s][kind, 0, rows, :]
                else:
                    outs[r][s, 0, kind] = held[s + kind][0, rows, :]


def serve_plane(sizes, wanted, pos, held):
    mates = sizes[0] * sizes[2]
    _, heads, rows, _ = held[0].shape
    pair = pl.BlockSpec((2, 1, rows, HD), lambda h, *_: (0, h, 0, 0))
    one = pl.BlockSpec((1, rows, HD), lambda h, *_: (h, 0, 0))
    return pl.pallas_call(
        functools.partial(serve_plane_kernel, sizes),
        out_shape=[jax.ShapeDtypeStruct((len(STEPS), heads, 2, KT, HD), held[0].dtype)] * mates,
        grid_spec=pltpu.PrefetchScalarGridSpec(
            num_scalar_prefetch=2,
            grid=(heads,),
            in_specs=[pair if h.ndim == 4 else one for h in held],
            out_specs=[pl.BlockSpec((len(STEPS), 1, 2, KT, HD), lambda h, *_: (0, h, 0, 0, 0))] * mates,
        ),
        compiler_params=LARGE,
    )(wanted, pos, *held)


def attend_kernel(tiles, parts, src_ref, dst_ref, num_ref, q_ref, do_ref, k_ref, v_ref, *refs):
    fars, (dq_ref, own_ref, out_ref, k_all, v_all, staged) = refs[:parts], refs[-6:]
    rows = q_ref.shape[1]
    total = rows + tiles * KT
    scale = HD**-0.5
    for h in range(GROUP):
        k_all[h, :rows] = k_ref[h]
        v_all[h, :rows] = v_ref[h]
        start = 0
        for far in fars:
            staged[h, start : start + far.shape[0]] = far[:, h]
            start += far.shape[0]
        for j in range(tiles):
            at = rows + j * KT
            k_all[h, at : at + KT] = staged[h, src_ref[j], 0]
            v_all[h, at : at + KT] = staged[h, src_ref[j], 1]

    row = lax.broadcasted_iota(jnp.int32, (total, rows), 0)
    inside = row < rows + num_ref[0] * KT
    for h in range(GROUP):
        q = q_ref[h]
        do = do_ref[:, h * HD : (h + 1) * HD]
        scores = lax.dot_general(
            k_all[h], q, (((1,), (1,)), ((), ())), preferred_element_type=jnp.float32
        )
        scores = jnp.where(inside, scores, -1e30)
        top = jnp.max(scores, axis=0, keepdims=True)
        weight = jnp.exp2((scores - top) * (scale * math.log2(math.e)))
        probs = weight * (1.0 / jnp.sum(weight, axis=0, keepdims=True))
        dprob = lax.dot_general(
            v_all[h], do, (((1,), (1,)), ((), ())), preferred_element_type=jnp.float32
        )
        delta = jnp.sum(probs * dprob, axis=0, keepdims=True)
        dscore = (probs * (dprob - delta) * scale).astype(jnp.bfloat16)
        probs_b = probs.astype(jnp.bfloat16)
        dq_ref[h] = lax.dot_general(
            k_all[h], dscore, (((0,), (0,)), ((), ())), preferred_element_type=jnp.float32
        ).T.astype(jnp.bfloat16)
        for kind, (left, right) in enumerate(((dscore, q), (probs_b, do))):
            part = jnp.dot(left, right, preferred_element_type=jnp.float32)
            own_ref[kind, h] = part[:rows]
            far = part[rows:].astype(jnp.bfloat16)
            for j in range(tiles):
                out_ref[dst_ref[j], h, kind] = far[j * KT : (j + 1) * KT]


def attend(src, dst, num, q, do, keys, values, fars, slots, first, earlier=()):
    heads, rows, _ = q.shape
    tiles = src.shape[0]
    held = sum(far.shape[0] for far in fars)
    total = rows + tiles * KT
    start = first // GROUP
    own = pl.BlockSpec((GROUP, rows, HD), lambda g, *_: (start + g, 0, 0))
    return pl.pallas_call(
        functools.partial(attend_kernel, tiles, len(fars)),
        out_shape=(
            jax.ShapeDtypeStruct((heads, rows, HD), jnp.bfloat16),
            jax.ShapeDtypeStruct((2, heads, rows, HD), jnp.float32),
            jax.ShapeDtypeStruct((slots, heads, 2, KT, HD), jnp.bfloat16),
        ),
        grid_spec=pltpu.PrefetchScalarGridSpec(
            num_scalar_prefetch=3,
            grid=(fars[0].shape[1] // GROUP,),
            in_specs=[own, pl.BlockSpec((rows, GROUP * HD), lambda g, *_: (0, start + g)), own, own]
            + [pl.BlockSpec((far.shape[0], GROUP, 2, KT, HD), lambda g, *_: (0, g, 0, 0, 0)) for far in fars]
            + [pl.BlockSpec(memory_space=pl.ANY)] * len(earlier),
            out_specs=(
                own,
                pl.BlockSpec((2, GROUP, rows, HD), lambda g, *_: (0, start + g, 0, 0)),
                pl.BlockSpec((slots, GROUP, 2, KT, HD), lambda g, *_: (0, start + g, 0, 0, 0)),
            ),
            scratch_shapes=[
                pltpu.VMEM((GROUP, total, HD), jnp.bfloat16),
                pltpu.VMEM((GROUP, total, HD), jnp.bfloat16),
                pltpu.VMEM((GROUP, held, 2, KT, HD), jnp.bfloat16),
            ],
        ),
        input_output_aliases={7 + len(fars) + i: i for i in range(len(earlier))},
        compiler_params=LARGE,
    )(src, dst, num, q, do, keys, values, *fars, *earlier)


def settle_kernel(asked_ref, own_ref, back_ref, dk_ref, dv_ref, *accs):
    slots, heads = back_ref.shape[:2]
    rows = own_ref.shape[2]
    for h in range(heads):
        for kind in range(2):
            accs[h * 2 + kind][:rows] = own_ref[kind, h]
    for s in range(slots):
        asked = asked_ref[s]
        at = tile_rows(jnp.where(asked >= 0, asked, rows // KT))
        for h in range(heads):
            for kind in range(2):
                accs[h * 2 + kind][at] += back_ref[s, h, kind].astype(jnp.float32)
    for h in range(heads):
        for kind, out in enumerate((dk_ref, dv_ref)):
            out[h] = accs[h * 2 + kind][:rows].astype(jnp.bfloat16)


def settle(asked, own, back, block=2):
    _, heads, rows, _ = own.shape
    slots = back.shape[0]
    out = pl.BlockSpec((block, rows, HD), lambda h, *_: (h, 0, 0))
    return pl.pallas_call(
        settle_kernel,
        out_shape=[jax.ShapeDtypeStruct((heads, rows, HD), jnp.bfloat16)] * 2,
        grid_spec=pltpu.PrefetchScalarGridSpec(
            num_scalar_prefetch=1,
            grid=(heads // block,),
            in_specs=[
                pl.BlockSpec((2, block, rows, HD), lambda h, *_: (0, h, 0, 0)),
                pl.BlockSpec((slots, block, 2, KT, HD), lambda h, *_: (0, h, 0, 0, 0)),
            ],
            out_specs=[out, out],
            scratch_shapes=[pltpu.VMEM((rows + KT, HD), jnp.float32)] * (2 * block),
        ),
        compiler_params=SMALL,
    )(asked, own, back)


def project_kernel(me_ref, own_ref, flip_ref, both_ref, w_ref, out_ref, acc):
    step = pl.program_id(0)

    def add(rows):
        part = lax.dot_general(rows, w_ref[...], (((1,), (1,)), ((), ())), preferred_element_type=jnp.float32)
        acc[...] = jnp.where(step == 0, part, acc[...] + part)

    @pl.when(step == 0)
    def _():
        add(own_ref[...])

    @pl.when(step == 1)
    def _():
        add(flip_ref[...])

    @pl.when(step == 2)
    def _():
        add(both_ref[0])

    @pl.when(step == 3)
    def _():
        add(both_ref[1])
        out_ref[...] = acc[...].astype(out_ref.dtype)


def columns(grad_out):
    swap = [(0, 1), (1, 0)]
    flip = lax.ppermute(grad_out, HEAD[0], swap)
    return flip, lax.ppermute(jnp.stack([grad_out, flip]), HEAD[1], swap)


def project(grad_out, flip, both, w_out):
    rows, width = grad_out.shape
    out_width = w_out.shape[0]
    me = (lax.axis_index(HEAD[0]) * 2 + lax.axis_index(HEAD[1])).astype(jnp.int32).reshape(1)
    block = lambda i, m: (0, m[0] ^ (i // 2 + (i % 2) * 2))
    return pl.pallas_call(
        project_kernel,
        out_shape=jax.ShapeDtypeStruct((rows, out_width), jnp.bfloat16),
        grid_spec=pltpu.PrefetchScalarGridSpec(
            num_scalar_prefetch=1,
            grid=(4,),
            in_specs=[
                pl.BlockSpec((rows, width), lambda i, m: (0, 0)),
                pl.BlockSpec((rows, width), lambda i, m: (0, 0)),
                pl.BlockSpec((2, rows, width), lambda i, m: (0, 0, 0)),
                pl.BlockSpec((out_width, width), block),
            ],
            out_specs=pl.BlockSpec((rows, out_width), lambda i, m: (0, 0)),
            scratch_shapes=[pltpu.VMEM((rows, out_width), jnp.float32)],
        ),
        compiler_params=LARGE,
    )(me, grad_out, flip, both, w_out)


def along_z(value, step):
    count = lax.axis_size("z")
    return lax.ppermute(value, "z", [(i, (i + step) % count) for i in range(count)])


def across_plane(value, dx, dy):
    nx, ny = lax.axis_size("x_lo"), lax.axis_size("y")
    pairs = [(x * ny + y, (x + dx) % nx * ny + (y + dy) % ny) for x in range(nx) for y in range(ny)]
    return lax.ppermute(value, PLANE, pairs)


def shards(queries, keys, values, grad_out, w_out, crit):
    queries, keys, values = (a.transpose(1, 0, 2) for a in (queries, keys, values))
    heads, rows, _ = queries.shape
    tiles_here = rows // KT
    sizes = tuple(lax.axis_size(a) for a in TOK)
    nx, nz, ny = sizes
    count = nx * nz * ny
    x, z, y = (lax.axis_index(a).astype(jnp.int32) for a in TOK)
    pos = jnp.stack([x, z, y])
    place = (x * nz + z) * ny + y

    entries = jnp.concatenate([crit[0], jnp.stack([place * tiles_here - 1, (place + 1) * tiles_here])])
    used = (entries >= 0) & (entries < count * tiles_here)
    owner = jnp.where(used, entries // tiles_here, place)
    blocks = jnp.arange(count)
    want = jnp.max(
        jnp.where(used[None, :] & (owner[None, :] == blocks[:, None]), entries[None, :] % tiles_here, -1), axis=1
    )
    wanted = lax.all_to_all(
        want.reshape(nx, nz, ny).transpose(0, 2, 1).reshape(nx * ny, nz), PLANE, 0, 0, tiled=True
    )
    asked = lax.all_to_all(wanted.T, "z", 0, 0, tiled=True)
    asked = asked.reshape(nz, nx, ny).transpose(1, 0, 2).reshape(count)
    wanted = wanted.reshape(nx * ny * nz)

    ring = jnp.stack([keys[:RING], values[:RING]])
    up, down = along_z(ring, 1), along_z(ring, -1)
    held = [ring, up, down]
    up, down, wanted = lax.optimization_barrier((up, down, wanted))
    up, down = along_z(up, 1), along_z(down, -1)
    held += [up, down]
    up, down, asked = lax.optimization_barrier((up, down, asked))
    up, down = along_z(up, 1), along_z(down, -1)
    held += [up, down]
    held += [along_z(up[0], 1), along_z(down[1], -1)]

    flip, both = columns(grad_out)

    tiles = entries.shape[0]
    order = jnp.arange(tiles)
    rank = jnp.sum(used[None, :] & (order[None, :] < order[:, None]), axis=1)
    slot = jnp.max(jnp.where(used[None, :] & (rank[None, :] == order[:, None]), owner[None, :], -1), axis=1)
    slot = jnp.where(slot >= 0, slot, place).astype(jnp.int32)
    number = jnp.sum(used.astype(jnp.int32)).reshape(1)
    dx, dz, dy = (x - slot // (nz * ny)) % nx, (slot // ny - z) % nz, (y - slot % ny) % ny
    rank_of = sum(jnp.where(dz == step % nz, s, 0) for s, step in enumerate(STEPS))
    plane_slot = ((dx * ny + dy) * len(STEPS) + rank_of).astype(jnp.int32)

    served = serve_all(asked, keys, values, RING)
    served, held, flip, both = lax.optimization_barrier((served, held, flip, both))
    far = lax.all_to_all(served, TOK, 0, 0, tiled=True)
    d_attn = project(grad_out, flip, both, w_out)
    held, d_attn = lax.optimization_barrier((held, d_attn))
    near = serve_plane(sizes, wanted, pos, held)
    near = [near[0]] + [across_plane(near[r], r // ny, r % ny) for r in range(1, nx * ny)]

    done = attend(slot, slot, number, queries, d_attn, keys, values, [far], count, RING)
    grad_q, own, out = attend(plane_slot, slot, number, queries, d_attn, keys, values, near, count, 0, done)
    back = lax.all_to_all(out, TOK, 0, 0, tiled=True)
    grad_k, grad_v = settle(asked, own, back)
    return tuple(a.transpose(1, 0, 2) for a in (grad_q, grad_k, grad_v))


def solution(mesh):
    fine = Mesh(mesh.devices.reshape(2, 8, 4, 2, 2), TOK + HEAD)
    return jax.shard_map(
        shards,
        mesh=fine,
        in_specs=(
            P(TOK, HEAD, None),
            P(TOK, HEAD, None),
            P(TOK, HEAD, None),
            P(TOK, HEAD),
            P(HEAD, None),
            P(TOK, None),
        ),
        out_specs=(P(TOK, HEAD, None), P(TOK, HEAD, None), P(TOK, HEAD, None)),
        check_vma=False,
    )
```

```python
import functools
import math

import jax
import jax.numpy as jnp
from jax import lax
from jax.experimental import pallas as pl
from jax.experimental.pallas import tpu as pltpu
from jax.sharding import Mesh
from jax.sharding import PartitionSpec as P

KT = 16
HD = 128
TOK = ("x_lo", "z", "y")
PLANE = ("x_lo", "y")
HEAD = ("x_hi", "core")
MIB = 1024 * 1024
RING = 3
STEPS = (0, -1, 1, -2, 2, -3, 3, 4)
GROUP = 1
PIECE = 8
SMALL = pltpu.CompilerParams(vmem_limit_bytes=16 * MIB)
LARGE = pltpu.CompilerParams(vmem_limit_bytes=60 * MIB)


def tile_rows(tile):
    return pl.ds(pl.multiple_of(tile * KT, KT), KT)


def serve_all_kernel(first, asked_ref, k_ref, v_ref, out_ref):
    block, heads = out_ref.shape[:2]
    for i in range(block):
        rows = tile_rows(jnp.maximum(asked_ref[pl.program_id(0) * block + i], 0))
        for h in range(heads):
            out_ref[i, h, 0] = k_ref[first + h, rows, :]
            out_ref[i, h, 1] = v_ref[first + h, rows, :]


def serve_all(asked, keys, values, first, block=16):
    count, heads = asked.shape[0], keys.shape[0] - first
    whole = pl.BlockSpec(keys.shape, lambda i, a: (0, 0, 0))
    return pl.pallas_call(
        functools.partial(serve_all_kernel, first),
        out_shape=jax.ShapeDtypeStruct((count, heads, 2, KT, HD), keys.dtype),
        grid_spec=pltpu.PrefetchScalarGridSpec(
            num_scalar_prefetch=1,
            grid=(count // block,),
            in_specs=[whole, whole],
            out_specs=pl.BlockSpec((block, heads, 2, KT, HD), lambda i, a: (i, 0, 0, 0, 0)),
        ),
        compiler_params=SMALL,
    )(asked, keys, values)


def serve_plane_kernel(sizes, wanted_ref, pos_ref, *refs):
    nx, nz, ny = sizes
    held, outs = refs[: -nx * ny], refs[-nx * ny :]
    for r in range(nx * ny):
        mate = lax.rem(pos_ref[0] + r // ny, nx) * ny + lax.rem(pos_ref[2] + r % ny, ny)
        for s, step in enumerate(STEPS):
            tile = wanted_ref[mate * nz + lax.rem(pos_ref[1] + step + nz, nz)]
            rows = tile_rows(jnp.maximum(tile, 0))
            for kind in range(2):
                if s < len(STEPS) - 1:
                    outs[r][s, 0, kind] = held[s][kind, 0, rows, :]
                else:
                    outs[r][s, 0, kind] = held[s + kind][0, rows, :]


def serve_plane(sizes, wanted, pos, held):
    mates = sizes[0] * sizes[2]
    _, heads, rows, _ = held[0].shape
    pair = pl.BlockSpec((2, 1, rows, HD), lambda h, *_: (0, h, 0, 0))
    one = pl.BlockSpec((1, rows, HD), lambda h, *_: (h, 0, 0))
    return pl.pallas_call(
        functools.partial(serve_plane_kernel, sizes),
        out_shape=[jax.ShapeDtypeStruct((len(STEPS), heads, 2, KT, HD), held[0].dtype)] * mates,
        grid_spec=pltpu.PrefetchScalarGridSpec(
            num_scalar_prefetch=2,
            grid=(heads,),
            in_specs=[pair if h.ndim == 4 else one for h in held],
            out_specs=[pl.BlockSpec((len(STEPS), 1, 2, KT, HD), lambda h, *_: (0, h, 0, 0, 0))] * mates,
        ),
        compiler_params=LARGE,
    )(wanted, pos, *held)


def attend_kernel(tiles, parts, list_ref, q_ref, do_ref, k_ref, v_ref, *refs):
    fars, (dq_ref, own_ref, out_ref, k_all, v_all, staged) = refs[:parts], refs[-6:]
    rows = q_ref.shape[1]
    total = rows + tiles * KT
    scale = HD**-0.5
    for h in range(GROUP):
        k_all[h, :rows] = k_ref[h]
        v_all[h, :rows] = v_ref[h]
        start = 0
        for far in fars:
            staged[h, start : start + far.shape[0]] = far[:, h]
            start += far.shape[0]
        for j in range(tiles):
            at = rows + j * KT
            k_all[h, at : at + KT] = staged[h, list_ref[j], 0]
            v_all[h, at : at + KT] = staged[h, list_ref[j], 1]

    row = lax.broadcasted_iota(jnp.int32, (total, rows), 0)
    inside = row < rows + list_ref[2 * tiles] * KT
    for h in range(GROUP):
        q = q_ref[h]
        do = do_ref[:, h * HD : (h + 1) * HD]
        scores = lax.dot_general(
            k_all[h], q, (((1,), (1,)), ((), ())), preferred_element_type=jnp.float32
        )
        scores = jnp.where(inside, scores, -1e30)
        top = jnp.max(scores, axis=0, keepdims=True)
        weight = jnp.exp2((scores - top) * (scale * math.log2(math.e)))
        probs = weight * (1.0 / jnp.sum(weight, axis=0, keepdims=True))
        dprob = lax.dot_general(
            v_all[h], do, (((1,), (1,)), ((), ())), preferred_element_type=jnp.float32
        )
        delta = jnp.sum(probs * dprob, axis=0, keepdims=True)
        dscore = (probs * (dprob - delta) * scale).astype(jnp.bfloat16)
        probs_b = probs.astype(jnp.bfloat16)
        dq_ref[h] = lax.dot_general(
            k_all[h], dscore, (((0,), (0,)), ((), ())), preferred_element_type=jnp.float32
        ).T.astype(jnp.bfloat16)
        for kind, (left, right) in enumerate(((dscore, q), (probs_b, do))):
            part = jnp.dot(left, right, preferred_element_type=jnp.float32)
            own_ref[kind, h] = part[:rows]
            far = part[rows:].astype(jnp.bfloat16)
            for j in range(tiles):
                out_ref[list_ref[tiles + j], h, kind] = far[j * KT : (j + 1) * KT]


def attend(listed, tiles, q, do, keys, values, fars, slots, first, earlier=()):
    heads, rows, _ = q.shape
    held = sum(far.shape[0] for far in fars)
    piece = lambda i: pl.BlockSpec((PIECE, GROUP, 2, KT, HD), lambda g, *_: (i, g, 0, 0, 0))
    pieces = [(far, piece(i)) for far in fars for i in range(far.shape[0] // PIECE)]
    total = rows + tiles * KT
    start = first // GROUP
    own = pl.BlockSpec((GROUP, rows, HD), lambda g, *_: (start + g, 0, 0))
    return pl.pallas_call(
        functools.partial(attend_kernel, tiles, len(pieces)),
        out_shape=(
            jax.ShapeDtypeStruct((heads, rows, HD), jnp.bfloat16),
            jax.ShapeDtypeStruct((2, heads, rows, HD), jnp.float32),
            jax.ShapeDtypeStruct((slots, heads, 2, KT, HD), jnp.bfloat16),
        ),
        grid_spec=pltpu.PrefetchScalarGridSpec(
            num_scalar_prefetch=1,
            grid=(fars[0].shape[1] // GROUP,),
            in_specs=[own, pl.BlockSpec((rows, GROUP * HD), lambda g, *_: (0, start + g)), own, own]
            + [spec for _, spec in pieces]
            + [pl.BlockSpec(memory_space=pl.ANY)] * len(earlier),
            out_specs=(
                own,
                pl.BlockSpec((2, GROUP, rows, HD), lambda g, *_: (0, start + g, 0, 0)),
                pl.BlockSpec((slots, GROUP, 2, KT, HD), lambda g, *_: (0, start + g, 0, 0, 0)),
            ),
            scratch_shapes=[
                pltpu.VMEM((GROUP, total, HD), jnp.bfloat16),
                pltpu.VMEM((GROUP, total, HD), jnp.bfloat16),
                pltpu.VMEM((GROUP, held, 2, KT, HD), jnp.bfloat16),
            ],
        ),
        input_output_aliases={5 + len(pieces) + i: i for i in range(len(earlier))},
        compiler_params=LARGE,
    )(listed, q, do, keys, values, *[far for far, _ in pieces], *earlier)


def settle_kernel(asked_ref, own_ref, back_ref, dk_ref, dv_ref, *accs):
    slots, heads = back_ref.shape[:2]
    rows = own_ref.shape[2]
    for h in range(heads):
        for kind in range(2):
            accs[h * 2 + kind][:rows] = own_ref[kind, h]
    for s in range(slots):
        asked = asked_ref[s]
        at = tile_rows(jnp.where(asked >= 0, asked, rows // KT))
        for h in range(heads):
            for kind in range(2):
                accs[h * 2 + kind][at] += back_ref[s, h, kind].astype(jnp.float32)
    for h in range(heads):
        for kind, out in enumerate((dk_ref, dv_ref)):
            out[h] = accs[h * 2 + kind][:rows].astype(jnp.bfloat16)


def settle(asked, own, back, block=2):
    _, heads, rows, _ = own.shape
    slots = back.shape[0]
    out = pl.BlockSpec((block, rows, HD), lambda h, *_: (h, 0, 0))
    return pl.pallas_call(
        settle_kernel,
        out_shape=[jax.ShapeDtypeStruct((heads, rows, HD), jnp.bfloat16)] * 2,
        grid_spec=pltpu.PrefetchScalarGridSpec(
            num_scalar_prefetch=1,
            grid=(heads // block,),
            in_specs=[
                pl.BlockSpec((2, block, rows, HD), lambda h, *_: (0, h, 0, 0)),
                pl.BlockSpec((slots, block, 2, KT, HD), lambda h, *_: (0, h, 0, 0, 0)),
            ],
            out_specs=[out, out],
            scratch_shapes=[pltpu.VMEM((rows + KT, HD), jnp.float32)] * (2 * block),
        ),
        compiler_params=SMALL,
    )(asked, own, back)


def project_kernel(me_ref, own_ref, flip_ref, both_ref, w_ref, out_ref, acc):
    step = pl.program_id(0)

    def add(rows):
        part = lax.dot_general(rows, w_ref[...], (((1,), (1,)), ((), ())), preferred_element_type=jnp.float32)
        acc[...] = jnp.where(step == 0, part, acc[...] + part)

    @pl.when(step == 0)
    def _():
        add(own_ref[...])

    @pl.when(step == 1)
    def _():
        add(flip_ref[...])

    @pl.when(step == 2)
    def _():
        add(both_ref[0])

    @pl.when(step == 3)
    def _():
        add(both_ref[1])
        out_ref[...] = acc[...].astype(out_ref.dtype)


def columns(grad_out):
    swap = [(0, 1), (1, 0)]
    flip = lax.ppermute(grad_out, HEAD[0], swap)
    return flip, lax.ppermute(jnp.stack([grad_out, flip]), HEAD[1], swap)


def project(grad_out, flip, both, w_out):
    rows, width = grad_out.shape
    out_width = w_out.shape[0]
    me = (lax.axis_index(HEAD[0]) * 2 + lax.axis_index(HEAD[1])).astype(jnp.int32).reshape(1)
    block = lambda i, m: (0, m[0] ^ (i // 2 + (i % 2) * 2))
    return pl.pallas_call(
        project_kernel,
        out_shape=jax.ShapeDtypeStruct((rows, out_width), jnp.bfloat16),
        grid_spec=pltpu.PrefetchScalarGridSpec(
            num_scalar_prefetch=1,
            grid=(4,),
            in_specs=[
                pl.BlockSpec((rows, width), lambda i, m: (0, 0)),
                pl.BlockSpec((rows, width), lambda i, m: (0, 0)),
                pl.BlockSpec((2, rows, width), lambda i, m: (0, 0, 0)),
                pl.BlockSpec((out_width, width), block),
            ],
            out_specs=pl.BlockSpec((rows, out_width), lambda i, m: (0, 0)),
            scratch_shapes=[pltpu.VMEM((rows, out_width), jnp.float32)],
        ),
        compiler_params=LARGE,
    )(me, grad_out, flip, both, w_out)


def along_z(value, step):
    count = lax.axis_size("z")
    return lax.ppermute(value, "z", [(i, (i + step) % count) for i in range(count)])


def across_plane(value, dx, dy):
    nx, ny = lax.axis_size("x_lo"), lax.axis_size("y")
    pairs = [(x * ny + y, (x + dx) % nx * ny + (y + dy) % ny) for x in range(nx) for y in range(ny)]
    return lax.ppermute(value, PLANE, pairs)


def shards(queries, keys, values, grad_out, w_out, crit):
    queries, keys, values = (a.transpose(1, 0, 2) for a in (queries, keys, values))
    heads, rows, _ = queries.shape
    tiles_here = rows // KT
    sizes = tuple(lax.axis_size(a) for a in TOK)
    nx, nz, ny = sizes
    count = nx * nz * ny
    x, z, y = (lax.axis_index(a).astype(jnp.int32) for a in TOK)
    pos = jnp.stack([x, z, y])
    place = (x * nz + z) * ny + y

    entries = jnp.concatenate([crit[0], jnp.stack([place * tiles_here - 1, (place + 1) * tiles_here])])
    used = (entries >= 0) & (entries < count * tiles_here)
    owner = jnp.where(used, entries // tiles_here, place)
    blocks = jnp.arange(count)
    want = jnp.max(
        jnp.where(used[None, :] & (owner[None, :] == blocks[:, None]), entries[None, :] % tiles_here, -1), axis=1
    )
    wanted = lax.all_to_all(
        want.reshape(nx, nz, ny).transpose(0, 2, 1).reshape(nx * ny, nz), PLANE, 0, 0, tiled=True
    )
    asked = lax.all_to_all(wanted.T, "z", 0, 0, tiled=True)
    asked = asked.reshape(nz, nx, ny).transpose(1, 0, 2).reshape(count)
    wanted = wanted.reshape(nx * ny * nz)

    ring = jnp.stack([keys[:RING], values[:RING]])
    up, down = along_z(ring, 1), along_z(ring, -1)
    held = [ring, up, down]
    up, down, wanted = lax.optimization_barrier((up, down, wanted))
    up, down = along_z(up, 1), along_z(down, -1)
    held += [up, down]
    up, down, asked = lax.optimization_barrier((up, down, asked))
    up, down = along_z(up, 1), along_z(down, -1)
    held += [up, down]
    held += [along_z(up[0], 1), along_z(down[1], -1)]

    flip, both = columns(grad_out)

    tiles = entries.shape[0]
    order = jnp.arange(tiles)
    rank = jnp.sum(used[None, :] & (order[None, :] < order[:, None]), axis=1)
    slot = jnp.max(jnp.where(used[None, :] & (rank[None, :] == order[:, None]), owner[None, :], -1), axis=1)
    slot = jnp.where(slot >= 0, slot, place).astype(jnp.int32)
    number = jnp.sum(used.astype(jnp.int32)).reshape(1)
    dx, dz, dy = (x - slot // (nz * ny)) % nx, (slot // ny - z) % nz, (y - slot % ny) % ny
    rank_of = sum(jnp.where(dz == step % nz, s, 0) for s, step in enumerate(STEPS))
    plane_slot = ((dx * ny + dy) * len(STEPS) + rank_of).astype(jnp.int32)

    served = serve_all(asked, keys, values, RING)
    served, held, flip, both = lax.optimization_barrier((served, held, flip, both))
    far = lax.all_to_all(served, TOK, 0, 0, tiled=True)
    d_attn = project(grad_out, flip, both, w_out)
    lists = [jnp.concatenate([src, slot, number]) for src in (slot, plane_slot)]
    held, d_attn, lists = lax.optimization_barrier((held, d_attn, lists))
    near = serve_plane(sizes, wanted, pos, held)
    near = [near[0]] + [across_plane(near[r], r // ny, r % ny) for r in range(1, nx * ny)]

    done = attend(lists[0], tiles, queries, d_attn, keys, values, [far], count, RING)
    grad_q, own, out = attend(lists[1], tiles, queries, d_attn, keys, values, near, count, 0, done)
    back = lax.all_to_all(out, TOK, 0, 0, tiled=True)
    grad_k, grad_v = settle(asked, own, back)
    return tuple(a.transpose(1, 0, 2) for a in (grad_q, grad_k, grad_v))


def solution(mesh):
    fine = Mesh(mesh.devices.reshape(2, 8, 4, 2, 2), TOK + HEAD)
    return jax.shard_map(
        shards,
        mesh=fine,
        in_specs=(
            P(TOK, HEAD, None),
            P(TOK, HEAD, None),
            P(TOK, HEAD, None),
            P(TOK, HEAD),
            P(HEAD, None),
            P(TOK, None),
        ),
        out_specs=(P(TOK, HEAD, None), P(TOK, HEAD, None), P(TOK, HEAD, None)),
        check_vma=False,
    )
```

```python
import functools
import math

import jax
import jax.numpy as jnp
from jax import lax
from jax.experimental import pallas as pl
from jax.experimental.pallas import tpu as pltpu
from jax.sharding import Mesh
from jax.sharding import PartitionSpec as P

KT = 16
HD = 128
TOK = ("x_lo", "z", "y")
PLANE = ("x_lo", "y")
HEAD = ("x_hi", "core")
MIB = 1024 * 1024
RING = 3
STEPS = (0, -1, 1, -2, 2, -3, 3, 4)
GROUP = 1
PIECE = 8
SMALL = pltpu.CompilerParams(vmem_limit_bytes=16 * MIB)
LARGE = pltpu.CompilerParams(vmem_limit_bytes=60 * MIB)


def tile_rows(tile):
    return pl.ds(pl.multiple_of(tile * KT, KT), KT)


def serve_all_kernel(first, asked_ref, k_ref, v_ref, out_ref):
    block, heads = out_ref.shape[:2]
    for i in range(block):
        rows = tile_rows(jnp.maximum(asked_ref[pl.program_id(0) * block + i], 0))
        for h in range(heads):
            out_ref[i, h, 0] = k_ref[first + h, rows, :]
            out_ref[i, h, 1] = v_ref[first + h, rows, :]


def serve_all(asked, keys, values, first, block=16):
    count, heads = asked.shape[0], keys.shape[0] - first
    whole = pl.BlockSpec(keys.shape, lambda i, a: (0, 0, 0))
    return pl.pallas_call(
        functools.partial(serve_all_kernel, first),
        out_shape=jax.ShapeDtypeStruct((count, heads, 2, KT, HD), keys.dtype),
        grid_spec=pltpu.PrefetchScalarGridSpec(
            num_scalar_prefetch=1,
            grid=(count // block,),
            in_specs=[whole, whole],
            out_specs=pl.BlockSpec((block, heads, 2, KT, HD), lambda i, a: (i, 0, 0, 0, 0)),
        ),
        compiler_params=SMALL,
    )(asked, keys, values)


def serve_plane_kernel(sizes, wanted_ref, pos_ref, *refs):
    nx, nz, ny = sizes
    held, outs = refs[: -nx * ny], refs[-nx * ny :]
    for r in range(nx * ny):
        mate = lax.rem(pos_ref[0] + r // ny, nx) * ny + lax.rem(pos_ref[2] + r % ny, ny)
        for s, step in enumerate(STEPS):
            tile = wanted_ref[mate * nz + lax.rem(pos_ref[1] + step + nz, nz)]
            rows = tile_rows(jnp.maximum(tile, 0))
            for kind in range(2):
                if s < len(STEPS) - 1:
                    outs[r][s, 0, kind] = held[s][kind, 0, rows, :]
                else:
                    outs[r][s, 0, kind] = held[s + kind][0, rows, :]


def serve_plane(sizes, wanted, pos, held):
    mates = sizes[0] * sizes[2]
    _, heads, rows, _ = held[0].shape
    pair = pl.BlockSpec((2, 1, rows, HD), lambda h, *_: (0, h, 0, 0))
    one = pl.BlockSpec((1, rows, HD), lambda h, *_: (h, 0, 0))
    return pl.pallas_call(
        functools.partial(serve_plane_kernel, sizes),
        out_shape=[jax.ShapeDtypeStruct((len(STEPS), heads, 2, KT, HD), held[0].dtype)] * mates,
        grid_spec=pltpu.PrefetchScalarGridSpec(
            num_scalar_prefetch=2,
            grid=(heads,),
            in_specs=[pair if h.ndim == 4 else one for h in held],
            out_specs=[pl.BlockSpec((len(STEPS), 1, 2, KT, HD), lambda h, *_: (0, h, 0, 0, 0))] * mates,
        ),
        compiler_params=LARGE,
    )(wanted, pos, *held)


def attend_kernel(tiles, parts, list_ref, q_ref, do_ref, k_ref, v_ref, *refs):
    fars, (dq_ref, own_ref, out_ref, k_all, v_all, staged) = refs[:parts], refs[-6:]
    rows = q_ref.shape[1]
    total = rows + tiles * KT
    scale = HD**-0.5
    for h in range(GROUP):
        k_all[h, :rows] = k_ref[h]
        v_all[h, :rows] = v_ref[h]
        start = 0
        for far in fars:
            staged[h, start : start + far.shape[0]] = far[:, h]
            start += far.shape[0]
        for j in range(tiles):
            at = rows + j * KT
            k_all[h, at : at + KT] = staged[h, list_ref[j], 0]
            v_all[h, at : at + KT] = staged[h, list_ref[j], 1]

    row = lax.broadcasted_iota(jnp.int32, (total, rows), 0)
    inside = row < rows + list_ref[2 * tiles] * KT
    for h in range(GROUP):
        q = q_ref[h]
        do = do_ref[:, h * HD : (h + 1) * HD]
        scores = lax.dot_general(
            k_all[h], q, (((1,), (1,)), ((), ())), preferred_element_type=jnp.float32
        )
        scores = jnp.where(inside, scores, -1e30)
        top = jnp.max(scores, axis=0, keepdims=True)
        weight = jnp.exp2((scores - top) * (scale * math.log2(math.e)))
        probs = weight * (1.0 / jnp.sum(weight, axis=0, keepdims=True))
        dprob = lax.dot_general(
            v_all[h], do, (((1,), (1,)), ((), ())), preferred_element_type=jnp.float32
        )
        delta = jnp.sum(probs * dprob, axis=0, keepdims=True)
        dscore = (probs * (dprob - delta) * scale).astype(jnp.bfloat16)
        probs_b = probs.astype(jnp.bfloat16)
        dq_ref[h] = lax.dot_general(
            k_all[h], dscore, (((0,), (0,)), ((), ())), preferred_element_type=jnp.float32
        ).T.astype(jnp.bfloat16)
        for kind, (left, right) in enumerate(((dscore, q), (probs_b, do))):
            part = jnp.dot(left, right, preferred_element_type=jnp.float32)
            own_ref[kind, h] = part[:rows]
            far = part[rows:].astype(jnp.bfloat16)
            for j in range(tiles):
                out_ref[list_ref[tiles + j], h, kind] = far[j * KT : (j + 1) * KT]


def attend(listed, tiles, q, do, keys, values, fars, slots, first, earlier=()):
    heads, rows, _ = q.shape
    held = sum(far.shape[0] for far in fars)
    piece = lambda i: pl.BlockSpec((PIECE, GROUP, 2, KT, HD), lambda g, *_: (i, g, 0, 0, 0))
    pieces = [(far, piece(i)) for far in fars for i in range(far.shape[0] // PIECE)]
    total = rows + tiles * KT
    start = first // GROUP
    own = pl.BlockSpec((GROUP, rows, HD), lambda g, *_: (start + g, 0, 0))
    return pl.pallas_call(
        functools.partial(attend_kernel, tiles, len(pieces)),
        out_shape=(
            jax.ShapeDtypeStruct((heads, rows, HD), jnp.bfloat16),
            jax.ShapeDtypeStruct((2, heads, rows, HD), jnp.float32),
            jax.ShapeDtypeStruct((slots, heads, 2, KT, HD), jnp.bfloat16),
        ),
        grid_spec=pltpu.PrefetchScalarGridSpec(
            num_scalar_prefetch=1,
            grid=(fars[0].shape[1] // GROUP,),
            in_specs=[own, pl.BlockSpec((rows, GROUP * HD), lambda g, *_: (0, start + g)), own, own]
            + [spec for _, spec in pieces]
            + [pl.BlockSpec(memory_space=pl.ANY)] * len(earlier),
            out_specs=(
                own,
                pl.BlockSpec((2, GROUP, rows, HD), lambda g, *_: (0, start + g, 0, 0)),
                pl.BlockSpec((slots, GROUP, 2, KT, HD), lambda g, *_: (0, start + g, 0, 0, 0)),
            ),
            scratch_shapes=[
                pltpu.VMEM((GROUP, total, HD), jnp.bfloat16),
                pltpu.VMEM((GROUP, total, HD), jnp.bfloat16),
                pltpu.VMEM((GROUP, held, 2, KT, HD), jnp.bfloat16),
            ],
        ),
        input_output_aliases={5 + len(pieces) + i: i for i in range(len(earlier))},
        compiler_params=LARGE,
    )(listed, q, do, keys, values, *[far for far, _ in pieces], *earlier)


def settle_kernel(asked_ref, own_ref, back_ref, dk_ref, dv_ref, *accs):
    slots = back_ref.shape[0]
    block, rows, _ = dk_ref.shape
    first = pl.program_id(0) * block
    for h in range(block):
        for kind in range(2):
            accs[h * 2 + kind][:rows] = own_ref[kind, first + h]
    for s in range(slots):
        asked = asked_ref[s]
        at = tile_rows(jnp.where(asked >= 0, asked, rows // KT))
        for h in range(block):
            for kind in range(2):
                accs[h * 2 + kind][at] += back_ref[s, first + h, kind].astype(jnp.float32)
    for h in range(block):
        for kind, out in enumerate((dk_ref, dv_ref)):
            out[h] = accs[h * 2 + kind][:rows].astype(jnp.bfloat16)


def settle(asked, own, back, block=2):
    _, heads, rows, _ = own.shape
    out = pl.BlockSpec((block, rows, HD), lambda h, *_: (h, 0, 0))
    return pl.pallas_call(
        settle_kernel,
        out_shape=[jax.ShapeDtypeStruct((heads, rows, HD), jnp.bfloat16)] * 2,
        grid_spec=pltpu.PrefetchScalarGridSpec(
            num_scalar_prefetch=1,
            grid=(heads // block,),
            in_specs=[pl.BlockSpec(memory_space=pltpu.VMEM)] * 2,
            out_specs=[out, out],
            scratch_shapes=[pltpu.VMEM((rows + KT, HD), jnp.float32)] * (2 * block),
        ),
        compiler_params=SMALL,
    )(asked, own, back)


def project_kernel(me_ref, own_ref, flip_ref, both_ref, w_ref, out_ref, acc):
    step = pl.program_id(0)

    def add(rows):
        part = lax.dot_general(rows, w_ref[...], (((1,), (1,)), ((), ())), preferred_element_type=jnp.float32)
        acc[...] = jnp.where(step == 0, part, acc[...] + part)

    @pl.when(step == 0)
    def _():
        add(own_ref[...])

    @pl.when(step == 1)
    def _():
        add(flip_ref[...])

    @pl.when(step == 2)
    def _():
        add(both_ref[0])

    @pl.when(step == 3)
    def _():
        add(both_ref[1])
        out_ref[...] = acc[...].astype(out_ref.dtype)


def columns(grad_out):
    swap = [(0, 1), (1, 0)]
    flip = lax.ppermute(grad_out, HEAD[0], swap)
    return flip, lax.ppermute(jnp.stack([grad_out, flip]), HEAD[1], swap)


def project(grad_out, flip, both, w_out):
    rows, width = grad_out.shape
    out_width = w_out.shape[0]
    me = (lax.axis_index(HEAD[0]) * 2 + lax.axis_index(HEAD[1])).astype(jnp.int32).reshape(1)
    block = lambda i, m: (0, m[0] ^ (i // 2 + (i % 2) * 2))
    return pl.pallas_call(
        project_kernel,
        out_shape=jax.ShapeDtypeStruct((rows, out_width), jnp.bfloat16),
        grid_spec=pltpu.PrefetchScalarGridSpec(
            num_scalar_prefetch=1,
            grid=(4,),
            in_specs=[
                pl.BlockSpec((rows, width), lambda i, m: (0, 0)),
                pl.BlockSpec((rows, width), lambda i, m: (0, 0)),
                pl.BlockSpec((2, rows, width), lambda i, m: (0, 0, 0)),
                pl.BlockSpec((out_width, width), block),
            ],
            out_specs=pl.BlockSpec((rows, out_width), lambda i, m: (0, 0)),
            scratch_shapes=[pltpu.VMEM((rows, out_width), jnp.float32)],
        ),
        compiler_params=LARGE,
    )(me, grad_out, flip, both, w_out)


def along_z(value, step):
    count = lax.axis_size("z")
    return lax.ppermute(value, "z", [(i, (i + step) % count) for i in range(count)])


def across_plane(value, dx, dy):
    nx, ny = lax.axis_size("x_lo"), lax.axis_size("y")
    pairs = [(x * ny + y, (x + dx) % nx * ny + (y + dy) % ny) for x in range(nx) for y in range(ny)]
    return lax.ppermute(value, PLANE, pairs)


def shards(queries, keys, values, grad_out, w_out, crit):
    queries, keys, values = (a.transpose(1, 0, 2) for a in (queries, keys, values))
    heads, rows, _ = queries.shape
    tiles_here = rows // KT
    sizes = tuple(lax.axis_size(a) for a in TOK)
    nx, nz, ny = sizes
    count = nx * nz * ny
    x, z, y = (lax.axis_index(a).astype(jnp.int32) for a in TOK)
    pos = jnp.stack([x, z, y])
    place = (x * nz + z) * ny + y

    entries = jnp.concatenate([crit[0], jnp.stack([place * tiles_here - 1, (place + 1) * tiles_here])])
    used = (entries >= 0) & (entries < count * tiles_here)
    owner = jnp.where(used, entries // tiles_here, place)
    blocks = jnp.arange(count)
    want = jnp.max(
        jnp.where(used[None, :] & (owner[None, :] == blocks[:, None]), entries[None, :] % tiles_here, -1), axis=1
    )
    wanted = lax.all_to_all(
        want.reshape(nx, nz, ny).transpose(0, 2, 1).reshape(nx * ny, nz), PLANE, 0, 0, tiled=True
    )
    asked = lax.all_to_all(wanted.T, "z", 0, 0, tiled=True)
    asked = asked.reshape(nz, nx, ny).transpose(1, 0, 2).reshape(count)
    wanted = wanted.reshape(nx * ny * nz)

    ring = jnp.stack([keys[:RING], values[:RING]])
    up, down = along_z(ring, 1), along_z(ring, -1)
    held = [ring, up, down]
    up, down, wanted = lax.optimization_barrier((up, down, wanted))
    up, down = along_z(up, 1), along_z(down, -1)
    held += [up, down]
    up, down, asked = lax.optimization_barrier((up, down, asked))
    up, down = along_z(up, 1), along_z(down, -1)
    held += [up, down]
    held += [along_z(up[0], 1), along_z(down[1], -1)]

    flip, both = columns(grad_out)

    tiles = entries.shape[0]
    order = jnp.arange(tiles)
    rank = jnp.sum(used[None, :] & (order[None, :] < order[:, None]), axis=1)
    slot = jnp.max(jnp.where(used[None, :] & (rank[None, :] == order[:, None]), owner[None, :], -1), axis=1)
    slot = jnp.where(slot >= 0, slot, place).astype(jnp.int32)
    number = jnp.sum(used.astype(jnp.int32)).reshape(1)
    dx, dz, dy = (x - slot // (nz * ny)) % nx, (slot // ny - z) % nz, (y - slot % ny) % ny
    rank_of = sum(jnp.where(dz == step % nz, s, 0) for s, step in enumerate(STEPS))
    plane_slot = ((dx * ny + dy) * len(STEPS) + rank_of).astype(jnp.int32)

    served = serve_all(asked, keys, values, RING)
    served, held, flip, both = lax.optimization_barrier((served, held, flip, both))
    far = lax.all_to_all(served, TOK, 0, 0, tiled=True)
    d_attn = project(grad_out, flip, both, w_out)
    lists = [jnp.concatenate([src, slot, number]) for src in (slot, plane_slot)]
    held, d_attn, lists = lax.optimization_barrier((held, d_attn, lists))
    near = serve_plane(sizes, wanted, pos, held)
    near = [near[0]] + [across_plane(near[r], r // ny, r % ny) for r in range(1, nx * ny)]

    done = attend(lists[0], tiles, queries, d_attn, keys, values, [far], count, RING)
    grad_q, own, out = attend(lists[1], tiles, queries, d_attn, keys, values, near, count, 0, done)
    back = lax.all_to_all(out, TOK, 0, 0, tiled=True)
    grad_k, grad_v = settle(asked, own, back)
    return tuple(a.transpose(1, 0, 2) for a in (grad_q, grad_k, grad_v))


def solution(mesh):
    fine = Mesh(mesh.devices.reshape(2, 8, 4, 2, 2), TOK + HEAD)
    return jax.shard_map(
        shards,
        mesh=fine,
        in_specs=(
            P(TOK, HEAD, None),
            P(TOK, HEAD, None),
            P(TOK, HEAD, None),
            P(TOK, HEAD),
            P(HEAD, None),
            P(TOK, None),
        ),
        out_specs=(P(TOK, HEAD, None), P(TOK, HEAD, None), P(TOK, HEAD, None)),
        check_vma=False,
    )
```
